512 devices in a mesh: ctx: 64 (over z_lo, y, core), section: 8 (over x, z_hi).
Axes of the slice: x: 4, y: 4, z: 16 (z_hi: 2, z_lo: 8; z = z_hi * 8 + z_lo), core: 2. Of those that a mesh axis runs over, the one named last changes fastest.
Arguments:
- gate: bfloat16 [8, 8192, 4096], P('section', 'ctx'), may hold values from -6 to 6
- grad_out: bfloat16 [8, 8192, 4096], P('section', 'ctx'), may hold values from -6 to 6
- decay: float32 [8, 16, 4096], P('section'), may hold values from 3.0517578e-05 to 0.0333333333, as said below
- amplitude: float32 [8, 16, 4096], P('section'), may hold values from -0.2581989 to 0.2581989, as said below
Outputs:
- passed: bfloat16 [8, 8192, 4096], P('section', 'ctx')
The draws below stay inside these ranges and needn't reach their ends.
Inputs may be any that keep to these rules, and one draw needn't show every extreme that they name: `decay`: decay rates per position of the filter's modes. `amplitude`: residues of the filter's modes.
All inputs are finite; a program needn't handle non-finite values.
Results may differ from the reference program's by a relative error of at most 0.0152.
Values may be sent and summed in bfloat16 or wider, within the bound.
No kernel may reach another device: no remote copies, remote signals or barrier semaphores. Data moves between devices by JAX's collectives and lax.ppermute only.
A program may use at most 128 MiB of HBM per device.

```python
import math
import jax
import jax.numpy as jnp
from jax import lax

D = 4096
MODES = 16
TOK_DEV = 128
TOKENS = 8192
SECTIONS = 8
N_CTX = 64


def draw_decay(key, part):
    key = jax.random.fold_in(key, 7)
    pick_key, slow_key, fast_key = jax.random.split(key, 3)
    grid_shape = (SECTIONS, MODES, D)
    slow_share = 0.5
    slow_mask = jax.random.uniform(pick_key, grid_shape) < slow_share
    rate_floor = 0.25 / TOKENS
    slow_top = 1.0 / TOKENS
    middle = 2.0 / TOKENS
    rate_top = 1.0 / 30.0
    slow_rate = rate_floor * (slow_top / rate_floor) ** jax.random.uniform(slow_key, grid_shape)
    fast_rate = middle * (rate_top / middle) ** jax.random.uniform(fast_key, grid_shape)
    return jnp.where(slow_mask, slow_rate, fast_rate).astype(jnp.float32)


def draw_amplitude(key, part):
    rates = draw_decay(key, part).astype(jnp.float32)
    key = jax.random.fold_in(key, 11)
    normal_part = jnp.clip(jax.random.normal(key, (SECTIONS, MODES, D), jnp.float32), -4.0, 4.0)
    weight_rate = jnp.maximum(rates, 1.0 / TOKENS)
    return (normal_part * jnp.sqrt(2.0 * weight_rate / MODES)).astype(jnp.float32)


def steps_of(key, extent, pieces, least, high):
    gain = 1.0
    for dim, shards_of in pieces:
        heights = jax.random.uniform(jax.random.fold_in(jax.random.fold_in(key, 6), dim), (shards_of,), jnp.float32, least / len(pieces), high / len(pieces))
        gain = gain * jnp.repeat(jnp.exp(heights), extent[dim] // shards_of).reshape((-1,) + (1,) * (len(extent) - 1 - dim))
    return gain


def normal_values(stream_key, dims, scale, bound, shards=(), kind=jnp.bfloat16):
    factor_of = steps_of(stream_key, dims, shards, -0.22, 0.18) if shards else 1.0
    values = jax.random.normal(stream_key, dims, jnp.float32) * scale * factor_of
    return jnp.minimum(jnp.maximum(values, -bound), bound).astype(kind)


def setup_inputs(seed: int = 0) -> dict:
    key_list = jax.random.split(jax.random.key(seed), 5)
    return {
        "gate": normal_values(key_list[0], (SECTIONS, TOKENS, D), 1.0, 6.0, ((0, 8), (1, 64))),
        "grad_out": normal_values(key_list[1], (SECTIONS, TOKENS, D), 1.0, 6.0, ((0, 8), (1, 64))),
        "decay": draw_decay(jax.random.fold_in(key_list[4], 71), 0),
        "amplitude": draw_amplitude(jax.random.fold_in(key_list[4], 71), 0),
    }


def unit_turn(step_index, period):
    residue = step_index % period
    nearest = jnp.minimum(residue, period - residue)
    angles = (2.0 * math.pi / period) * nearest.astype(jnp.float32)
    cos_tab = jnp.cos(angles)
    sin_tab = jnp.sin(angles)
    sin_tab = jnp.where(2 * residue > period, -sin_tab, sin_tab)
    sin_tab = jnp.where((residue == 0) | (2 * residue == period), 0.0, sin_tab)
    return cos_tab, sin_tab


def forward_rows(a_values, wide, blocks):
    cos_tab, sin_tab = unit_turn(a_values[:, None] * jnp.arange(blocks, dtype=jnp.int32)[None, :], wide)
    return jnp.stack([cos_tab, -sin_tab]).astype(jnp.bfloat16)


def inverse_rows(a_values, wide, blocks):
    cos_tab, sin_tab = unit_turn(jnp.arange(blocks, dtype=jnp.int32)[:, None] * a_values[None, :], wide)
    return jnp.stack([cos_tab, -sin_tab]).astype(jnp.bfloat16)


def column_tables(a_values, seq_rows, period, wide):
    offsets = jnp.arange(seq_rows, dtype=jnp.int32)
    freq_index = a_values[:, None] + wide * offsets[None, :]
    cos_tab, sin_tab = unit_turn(offsets[None, :, None] * freq_index[:, None, :], period)
    cos_tab = cos_tab.astype(jnp.bfloat16)
    sin_tab = sin_tab.astype(jnp.bfloat16)
    fwd_table = jnp.stack([jnp.stack([cos_tab, -sin_tab], axis=2), jnp.stack([sin_tab, cos_tab], axis=2)], axis=1)
    cos_back = jnp.swapaxes(cos_tab, 1, 2)
    sin_back = jnp.swapaxes(sin_tab, 1, 2)
    inv_table = jnp.stack([jnp.stack([cos_back, sin_back], axis=2), jnp.stack([-sin_back, cos_back], axis=2)], axis=1)
    return freq_index, fwd_table, inv_table


def filter_spectrum(frequency, decay_rate, mode_gain, length, block_size):
    period = 2 * length
    retain = jnp.exp(-decay_rate)
    leakage = -jnp.expm1(-decay_rate)
    end_decay = jnp.exp(-decay_rate * length)
    end_leak = -jnp.expm1(-decay_rate * length)

    def one_block(freq_block):
        residue = freq_block % period
        nearest = jnp.minimum(residue, period - residue)
        sin_tab = unit_turn(freq_block, period)[1]
        half_sine = jnp.sin((math.pi / period) * nearest.astype(jnp.float32))
        odd_freq = (residue % 2 == 1)[None, :, None]
        numerator = jnp.where(odd_freq, 1.0 + end_decay[:, None, :], end_leak[:, None, :])
        real_d = leakage[:, None, :] + 2.0 * retain[:, None, :] * (half_sine * half_sine)[None, :, None]
        imag_d = retain[:, None, :] * sin_tab[None, :, None]
        weighting = mode_gain[:, None, :] * numerator / (real_d * real_d + imag_d * imag_d)
        return jnp.sum(weighting * real_d, axis=0), -jnp.sum(weighting * imag_d, axis=0)

    real_part, imag_part = lax.map(one_block, frequency.reshape(-1, block_size))
    channels = decay_rate.shape[1]
    return real_part.reshape(-1, channels), imag_part.reshape(-1, channels)


def reference(gate, grad_out, decay, amplitude):
    blocks = N_CTX
    seq_rows = TOK_DEV
    wide = 2 * blocks
    length = seq_rows * blocks
    period = 2 * length
    highest = lax.Precision.HIGHEST

    def one_section(section_items):
        gate_part, grad_part, decay_rate, mode_gain = section_items
        gated_grad = (gate_part.astype(jnp.float32) * grad_part.astype(jnp.float32)).astype(jnp.bfloat16)
        spread = gated_grad.reshape(blocks, seq_rows, -1).astype(jnp.float32)
        a_values = jnp.arange(wide, dtype=jnp.int32)
        lifted = jnp.einsum("rap,pic->raic", forward_rows(a_values, wide, blocks).astype(jnp.float32), spread, precision=highest).astype(jnp.bfloat16)
        freq_index, fwd_table, inv_table = column_tables(a_values, seq_rows, period, wide)
        forward_spec = jnp.einsum("rxic,xriob->oxbc", lifted.astype(jnp.float32), fwd_table.astype(jnp.float32), precision=highest)
        real_h, imag_h = filter_spectrum(freq_index.reshape(-1), decay_rate, mode_gain, length, 2 * seq_rows)
        real_h = real_h.reshape(forward_spec.shape[1:])
        imag_h = imag_h.reshape(forward_spec.shape[1:])
        product = jnp.stack([(real_h * forward_spec[0] + imag_h * forward_spec[1]) / period, (real_h * forward_spec[1] - imag_h * forward_spec[0]) / period]).astype(jnp.bfloat16)
        partial_value = jnp.einsum("rxbc,xrboi->oxic", product.astype(jnp.float32), inv_table.astype(jnp.float32), precision=highest).astype(jnp.bfloat16)
        back_table = inverse_rows(a_values, wide, blocks)
        grad_rows = jnp.einsum("raic,rpa->pic", partial_value.astype(jnp.float32), back_table.astype(jnp.float32), precision=highest).astype(jnp.bfloat16)
        return grad_rows.reshape(length, -1)

    section_grads = lax.map(one_section, (gate, grad_out, decay, amplitude))
    return jnp.roll(section_grads, -1, axis=0)
```

```python
import functools

import jax
import jax.numpy as jnp
from jax import lax
from jax.experimental import pallas as pl
from jax.experimental.pallas import tpu as pltpu
from jax.sharding import Mesh, PartitionSpec as P

MODES = 16
ROWS = 128
CHIP_RUN = 8
F32 = jnp.float32


def gated_rows(gate, grad):
    return (gate.astype(F32) * grad.astype(F32)).astype(jnp.bfloat16).astype(F32)


def lanes_of(group):
    return pl.ds(pl.multiple_of(group * 128, 128), 128)


def spread(row):
    return jnp.broadcast_to(row, (8, 128))


def state_kernel(gate_ref, grad_ref, decay_ref, state_ref):
    sub = lax.broadcasted_iota(jnp.int32, (8, 128), 0).astype(F32)

    def one_group(group, _):
        lanes = lanes_of(group)
        rates = [spread(decay_ref[j : j + 1, lanes]) for j in range(MODES)]
        leap = [jnp.exp(-8.0 * r) for r in rates]
        held = [None] * MODES
        for pair in reversed(range(ROWS // 16)):
            rows = slice(16 * pair, 16 * pair + 16)
            both = gated_rows(gate_ref[rows, lanes], grad_ref[rows, lanes])
            for part in (both[8:16], both[0:8]):
                held = [part if h is None else h * q + part for h, q in zip(held, leap)]
        for j in range(MODES):
            total = jnp.sum(held[j] * jnp.exp(-rates[j] * sub), axis=0, keepdims=True)
            state_ref[j // 2, j % 2 : j % 2 + 1, lanes] = total
        return 0

    lax.fori_loop(0, state_ref.shape[2] // 128, one_group, 0)


def block_states(gate, grad, decay, width=1024):
    channels = gate.shape[1]
    wide = lambda c: (0, c)
    return pl.pallas_call(
        state_kernel,
        grid=(channels // width,),
        in_specs=[
            pl.BlockSpec((ROWS, width), wide),
            pl.BlockSpec((ROWS, width), wide),
            pl.BlockSpec((MODES, width), wide),
        ],
        out_specs=pl.BlockSpec((MODES // 2, 2, width), lambda c: (0, 0, c)),
        out_shape=jax.ShapeDtypeStruct((MODES // 2, 2, channels), F32),
        name="block_states",
    )(gate, grad, decay)


def plane_kernel(state_ref, rate_ref, total_ref):
    step = jnp.exp(-float(ROWS) * rate_ref[...])
    total = state_ref[CHIP_RUN - 1]
    for k in reversed(range(CHIP_RUN - 1)):
        total = total * step + state_ref[k]
    for k in range(CHIP_RUN):
        total_ref[k] = total


def plane_totals(states, rates):
    return pl.pallas_call(
        plane_kernel,
        out_shape=jax.ShapeDtypeStruct(states.shape, F32),
        name="plane_totals",
    )(states, rates)


def entry_kernel(plane_ref, state_ref, total_ref, rate_ref, entry_ref):
    plane = plane_ref[0]
    rates = rate_ref[...]
    step = jnp.exp(-float(ROWS) * rates)
    stride = jnp.exp(-float(ROWS * CHIP_RUN) * rates)
    carry = jnp.zeros_like(rates)
    for z in reversed(range(1, CHIP_RUN)):
        carry = jnp.where(z > plane, carry * stride + total_ref[z], carry)
    for k in reversed(range(CHIP_RUN)):
        entry_ref[k] = carry
        carry = carry * step + state_ref[k]


def block_entries(plane, states, totals, rates):
    whole = pl.BlockSpec(memory_space=pltpu.VMEM)
    return pl.pallas_call(
        entry_kernel,
        in_specs=[pl.BlockSpec(memory_space=pltpu.SMEM), whole, whole, whole],
        out_shape=jax.ShapeDtypeStruct(states.shape, F32),
        name="block_entries",
    )(plane, states, totals, rates)


def sweep_kernel(gate_ref, grad_ref, entry_ref, decay_ref, gain_ref, out_ref, source, result):
    sub = lax.broadcasted_iota(jnp.int32, (8, 128), 0)

    def one_group(group, _):
        lanes = lanes_of(group)
        for pair in range(ROWS // 16):
            rows = slice(16 * pair, 16 * pair + 16)
            source[rows, :] = gated_rows(gate_ref[rows, lanes], grad_ref[rows, lanes])
        rates = [spread(decay_ref[j : j + 1, lanes]) for j in range(MODES)]
        keep = [jnp.exp(-r) for r in rates]
        held = [None] * MODES
        for i in reversed(range(16)):
            part = source[pl.ds(i, 8, stride=16), :]
            held = [part if h is None else h * q + part for h, q in zip(held, keep)]
        for j in range(MODES):
            enter = spread(entry_ref[j // 2, j % 2 : j % 2 + 1, lanes])
            value = jnp.where(sub == 7, enter, pltpu.roll(held[j], 7, 0))
            for shift in (1, 2, 4):
                leap = jnp.where(sub < 8 - shift, jnp.exp(-16.0 * shift * rates[j]), 0.0)
                value = value + leap * pltpu.roll(value, 8 - shift, 0)
            held[j] = value
        gains = [spread(gain_ref[j : j + 1, lanes]) for j in range(MODES)]
        for i in reversed(range(16)):
            part = source[pl.ds(i, 8, stride=16), :]
            held = [h * q + part for h, q in zip(held, keep)]
            terms = [h * a for h, a in zip(held, gains)]
            while len(terms) > 1:
                terms = [a + b for a, b in zip(terms[::2], terms[1::2])]
            result[pl.ds(i, 8, stride=16), :] = terms[0]
        for pair in range(ROWS // 16):
            rows = slice(16 * pair, 16 * pair + 16)
            out_ref[rows, lanes] = result[rows, :].astype(jnp.bfloat16)
        return 0

    lax.fori_loop(0, out_ref.shape[1] // 128, one_group, 0)


def sweep(gate, grad, entries, decay, gain, width=1024):
    channels = gate.shape[1]
    wide = lambda c: (0, c)
    return pl.pallas_call(
        sweep_kernel,
        grid=(channels // width,),
        in_specs=[
            pl.BlockSpec((ROWS, width), wide),
            pl.BlockSpec((ROWS, width), wide),
            pl.BlockSpec((MODES // 2, 2, width), lambda c: (0, 0, c)),
            pl.BlockSpec((MODES, width), wide),
            pl.BlockSpec((MODES, width), wide),
        ],
        out_specs=pl.BlockSpec((ROWS, width), wide),
        out_shape=jax.ShapeDtypeStruct((ROWS, channels), jnp.bfloat16),
        scratch_shapes=[pltpu.VMEM((ROWS, 128), F32), pltpu.VMEM((ROWS, 128), F32)],
        name="sweep",
    )(gate, grad, entries, decay, gain)


def exchange(values, axis):
    return lax.all_to_all(values, axis, split_axis=0, concat_axis=0, tiled=True)


def passed_along(shard, axis, by):
    count = lax.axis_size(axis)
    return lax.ppermute(shard, axis, [(i, (i + by) % count) for i in range(count)])


def shards(gate, grad, decay, amplitude):
    gate, grad, decay, gain = gate[0], grad[0], decay[0], amplitude[0]
    place = lax.axis_index("place")
    plane = lax.axis_index("plane").reshape(1)
    own_rates = lax.dynamic_slice_in_dim(decay, 2 * place, 2, axis=0)
    states = exchange(block_states(gate, grad, decay), "place")
    totals = exchange(plane_totals(states, own_rates), "plane")
    entries = exchange(block_entries(plane, states, totals, own_rates), "place")
    local = sweep(gate, grad, entries, decay, gain)
    return passed_along(local, "section", -1)[None]


def solution(mesh):
    sections = mesh.shape["section"]
    parts = Mesh(
        mesh.devices.reshape(CHIP_RUN, CHIP_RUN, sections), ("plane", "place", "section")
    )
    rows = P("section", ("plane", "place"), None)
    params = P("section", None, None)
    return jax.shard_map(
        shards,
        mesh=parts,
        in_specs=(rows, rows, params, params),
        out_specs=rows,
        check_vma=False,
    )
```

```python
import functools

import jax
import jax.numpy as jnp
from jax import lax
from jax.experimental import pallas as pl
from jax.experimental.pallas import tpu as pltpu
from jax.sharding import Mesh, PartitionSpec as P

MODES = 16
ROWS = 128
PLACES = 8
SLOT = MODES // PLACES
PLANES = 64 // PLACES
EARLY = 2048
WIDTH = 1024
HALF = PLANES // 2
F32 = jnp.float32


def gated_rows(gate, grad):
    return (gate.astype(F32) * grad.astype(F32)).astype(jnp.bfloat16).astype(F32)


def lanes_of(group):
    return pl.ds(pl.multiple_of(group * 128, 128), 128)


def mode_row(ref, j, lanes):
    row = ref[j : j + 1, lanes] if len(ref.shape) == 2 else ref[j // SLOT, j % SLOT : j % SLOT + 1, lanes]
    return jnp.broadcast_to(row, (8, 128))


def source_rows(refs, rows, lanes):
    if len(refs) == 1:
        return refs[0][rows, lanes].astype(F32)
    return gated_rows(refs[0][rows, lanes], refs[1][rows, lanes])


def columns(shape, first=0):
    lead = (0,) * (len(shape) - 1)
    skip = first // WIDTH
    return pl.BlockSpec(shape[:-1] + (WIDTH,), lambda c: lead + (c + skip,))


def in_parts(kernel, sources, counts):
    def body(*refs):
        if len(counts) == 1:
            return kernel(refs[:sources], *refs[sources:])
        step, start = pl.program_id(0), 0
        for source, count in zip(refs[:sources], counts):
            pl.when((step >= start) & (step < start + count))(
                functools.partial(kernel, (source,), *refs[sources:])
            )
            start += count

    return body


def part_columns(parts):
    specs, start = [], 0
    for part in parts:
        count = part.shape[1] // WIDTH
        specs.append(
            pl.BlockSpec(
                (ROWS, WIDTH), lambda c, s=start, n=count: (0, jnp.clip(c - s, 0, n - 1))
            )
        )
        start += count
    return specs, [part.shape[1] // WIDTH for part in parts]


def state_kernel(sources, decay_ref, state_ref):
    sub = lax.broadcasted_iota(jnp.int32, (8, 128), 0).astype(F32)

    def one_group(group, _):
        lanes = lanes_of(group)
        rates = [mode_row(decay_ref, j, lanes) for j in range(MODES)]
        leap = [jnp.exp(-8.0 * r) for r in rates]
        held = [None] * MODES
        for pair in reversed(range(ROWS // 16)):
            both = source_rows(sources, slice(16 * pair, 16 * pair + 16), lanes)
            for part in (both[8:16], both[0:8]):
                held = [part if h is None else h * q + part for h, q in zip(held, leap)]
        for j in range(MODES):
            total = jnp.sum(held[j] * jnp.exp(-rates[j] * sub), axis=0, keepdims=True)
            state_ref[j // SLOT, j % SLOT : j % SLOT + 1, lanes] = total
        return 0

    lax.fori_loop(0, state_ref.shape[2] // 128, one_group, 0)


def all_states(gate, grad, decay, width=1024):
    channels = gate.shape[1]
    wide = lambda c: (0, c)
    return pl.pallas_call(
        in_parts(state_kernel, 2, [1]),
        grid=(channels // width,),
        in_specs=[pl.BlockSpec((n, width), wide) for n in (ROWS, ROWS, MODES)],
        out_specs=pl.BlockSpec((PLACES, SLOT, width), lambda c: (0, 0, c)),
        out_shape=jax.ShapeDtypeStruct((PLACES, SLOT, channels), F32),
        name="all_states",
    )(gate, grad, decay)


def early_states(parts, decay, decay_first):
    specs, counts = part_columns(parts)
    return pl.pallas_call(
        in_parts(state_kernel, len(parts), counts),
        grid=(sum(counts),),
        in_specs=specs + [columns(decay.shape, decay_first)],
        out_specs=columns((PLACES, SLOT, EARLY)),
        out_shape=jax.ShapeDtypeStruct((PLACES, SLOT, EARLY), F32),
        name="early_states",
    )(*parts, decay)


def plane_kernel(state_ref, rate_ref, gain_ref, sum_ref, full_ref, entry_ref):
    channels = rate_ref.shape[1]
    step = jnp.exp(-float(ROWS) * rate_ref[...])
    total = jnp.zeros_like(step)
    for k in reversed(range(PLACES)):
        entry_ref[k] = total[:, EARLY:]
        total = total * step + state_ref[k]
    for ref in (sum_ref, full_ref):
        ref[:, :EARLY] = total[:, :EARLY]
        ref[:, EARLY:channels] = total[:, EARLY:] * gain_ref[:, EARLY:]
    full_ref[:, channels : 2 * channels] = rate_ref[...]
    full_ref[:, 2 * channels :] = gain_ref[:, :EARLY]


def plane_sums(states, rates, gains):
    channels = rates.shape[1]
    return pl.pallas_call(
        plane_kernel,
        out_shape=[
            jax.ShapeDtypeStruct((SLOT, channels), F32),
            jax.ShapeDtypeStruct((SLOT, 2 * channels + EARLY), F32),
            jax.ShapeDtypeStruct((PLACES, SLOT, channels - EARLY), F32),
        ],
        name="plane_sums",
    )(states, rates, gains)


def entry_kernel(plane_ref, state_ref, full_ref, *refs):
    sum_refs, entry_ref = refs[:-1], refs[-1]
    channels = entry_ref.shape[2]
    rates = full_ref[:, channels : 2 * channels]
    stride = jnp.exp(-float(ROWS * PLACES) * rates)
    middle = jnp.where(plane_ref[0] < PLANES - HALF, full_ref[:, :channels], 0.0)
    values = [ref[...] for ref in sum_refs]
    values.insert(HALF - 1, middle)
    carry = values.pop()
    while values:
        carry = carry * stride + values.pop()
    step = jnp.exp(-float(ROWS) * rates)
    early, late = carry[:, :EARLY], carry[:, EARLY:]
    for k in reversed(range(PLACES)):
        entry_ref[k, :, :EARLY] = early
        entry_ref[k, :, EARLY:] = late
        early = early * step[:, :EARLY] + state_ref[k]
        late = late * step[:, EARLY:]


def block_entries(plane, states, full, sums):
    whole = pl.BlockSpec(memory_space=pltpu.VMEM)
    return pl.pallas_call(
        entry_kernel,
        in_specs=[pl.BlockSpec(memory_space=pltpu.SMEM)] + [whole] * (2 + len(sums)),
        out_shape=jax.ShapeDtypeStruct((PLACES, SLOT, sums[0].shape[1]), F32),
        name="block_entries",
    )(plane, states, full, *sums)


def sweep_kernel(sources, entry_ref, decay_ref, gain_ref, out_ref, source, result):
    sub = lax.broadcasted_iota(jnp.int32, (8, 128), 0)

    def one_group(group, _):
        lanes = lanes_of(group)
        for pair in range(ROWS // 16):
            rows = slice(16 * pair, 16 * pair + 16)
            source[rows, :] = source_rows(sources, rows, lanes)
        rates = [mode_row(decay_ref, j, lanes) for j in range(MODES)]
        keep = [jnp.exp(-r) for r in rates]
        held = [None] * MODES
        for i in reversed(range(16)):
            part = source[pl.ds(i, 8, stride=16), :]
            held = [part if h is None else h * q + part for h, q in zip(held, keep)]
        for j in range(MODES):
            value = jnp.where(sub == 7, mode_row(entry_ref, j, lanes), pltpu.roll(held[j], 7, 0))
            for shift in (1, 2, 4):
                leap = jnp.where(sub < 8 - shift, jnp.exp(-16.0 * shift * rates[j]), 0.0)
                value = value + leap * pltpu.roll(value, 8 - shift, 0)
            held[j] = value
        gains = [mode_row(gain_ref, j, lanes) for j in range(MODES)]
        for i in reversed(range(16)):
            part = source[pl.ds(i, 8, stride=16), :]
            held = [h * q + part for h, q in zip(held, keep)]
            terms = [h * a for h, a in zip(held, gains)]
            while len(terms) > 1:
                terms = [a + b for a, b in zip(terms[::2], terms[1::2])]
            result[pl.ds(i, 8, stride=16), :] = terms[0]
        for pair in range(ROWS // 16):
            rows = slice(16 * pair, 16 * pair + 16)
            out_ref[rows, lanes] = result[rows, :].astype(jnp.bfloat16)
        return 0

    lax.fori_loop(0, WIDTH // 128, one_group, 0)


def sweep(sources, specs, counts, params, channels, out_channels):
    return pl.pallas_call(
        in_parts(sweep_kernel, len(sources), counts),
        grid=(channels // WIDTH,),
        in_specs=specs + [columns(a.shape, first) for a, first in params],
        out_specs=columns((ROWS, out_channels)),
        out_shape=jax.ShapeDtypeStruct((ROWS, out_channels), jnp.bfloat16),
        scratch_shapes=[pltpu.VMEM((ROWS, 128), F32), pltpu.VMEM((ROWS, 128), F32)],
        name="sweep",
    )(*sources, *(a for a, _ in params))


def finish_kernel(_, late_ref, entry_ref, decay_ref, out_ref):
    ahead = 8.0 - lax.broadcasted_iota(jnp.int32, (8, 128), 0).astype(F32)

    def one_group(group, _):
        lanes = lanes_of(group)
        rates = [mode_row(decay_ref, j, lanes) for j in range(MODES)]
        leap = [jnp.exp(-8.0 * r) for r in rates]
        held = [
            mode_row(entry_ref, j, lanes) * jnp.exp(-r * ahead) for j, r in enumerate(rates)
        ]
        for pair in reversed(range(ROWS // 16)):
            rows = slice(16 * pair, 16 * pair + 16)
            halves = []
            for _ in range(2):
                terms = held
                while len(terms) > 1:
                    terms = [a + b for a, b in zip(terms[::2], terms[1::2])]
                halves.append(terms[0])
                held = [h * q for h, q in zip(held, leap)]
            whole = jnp.concatenate(halves[::-1], axis=0)
            out_ref[rows, lanes] = (late_ref[rows, lanes].astype(F32) + whole).astype(jnp.bfloat16)
        return 0

    lax.fori_loop(0, WIDTH // 128, one_group, 0)


def finish_late(out, late_rows, entries, decay):
    late = late_rows.shape[1]
    return pl.pallas_call(
        finish_kernel,
        grid=(late // WIDTH,),
        in_specs=[
            pl.BlockSpec(memory_space=pl.ANY),
            columns(late_rows.shape),
            columns(entries.shape, EARLY),
            columns(decay.shape, EARLY),
        ],
        out_specs=columns(out.shape, EARLY),
        out_shape=pltpu.HBM(out.shape, out.dtype),
        input_output_aliases={0: 0},
        name="finish_late",
    )(out, late_rows, entries, decay)


def exchange(values, axis):
    return lax.all_to_all(values, axis, split_axis=0, concat_axis=0, tiled=True)


def passed_along(shard, axis, by):
    count = lax.axis_size(axis)
    return lax.ppermute(shard, axis, [(i, (i + by) % count) for i in range(count)])


def as_one_step(always, step, *args):
    shapes = jax.eval_shape(step, *args)
    empty = lambda *_: jax.tree.map(lambda a: jnp.zeros(a.shape, a.dtype), shapes)
    return lax.cond(always, step, empty, *args)


def from_plane(message, by, ring):
    planes, sections = lax.axis_size("plane"), lax.axis_size("section")
    pairs = [
        (z * sections + s, (z - by) % planes * sections + (s - 1) % sections)
        for z in range(0 if ring else by, planes)
        for s in range(sections)
    ]
    return lax.ppermute(message, ("plane", "section"), pairs)


def late_step(gate, grad, decay, gain):
    late = gate.shape[1] - EARLY
    first = SLOT * lax.axis_index("place")
    rates = lax.dynamic_slice_in_dim(decay, first, SLOT, axis=0)
    gains = lax.dynamic_slice_in_dim(gain, first, SLOT, axis=0)
    states = exchange(all_states(gate, grad, decay), "place")
    total, full, entries = plane_sums(states, rates, gains)
    full = from_plane(full, HALF, True)
    sums = [from_plane(total, k, False) for k in range(1, HALF)]
    total, full, *sums = lax.optimization_barrier((total, full, *sums))
    sums += [from_plane(total, k, False) for k in range(HALF + 1, PLANES)]
    entries = exchange(entries, "place")
    sources = [gate, grad]
    specs = [columns(s.shape, EARLY) for s in sources]
    params = [(entries, 0), (decay, EARLY), (gain, EARLY)]
    return sweep(sources, specs, [1], params, late, late), full, sums


def early_step(plane, gated, full, sums):
    channels = sums[0].shape[1]
    specs, counts = part_columns([gated])
    params = jnp.broadcast_to(full[None, :, channels:], (PLACES, SLOT, channels + EARLY))
    params = exchange(params, "place")
    states = exchange(early_states([gated], params, 0), "place")
    entries = exchange(block_entries(plane, states, full, sums), "place")
    columns_of = [(entries, 0), (params, 0), (params, channels)]
    return sweep([gated], specs, counts, columns_of, EARLY, channels), entries, params


def shards(gate, grad, decay, amplitude):
    gate, grad, decay, gain = gate[0], grad[0], decay[0], amplitude[0]
    always = lax.axis_index("place") >= 0
    plane = lax.axis_index("plane").reshape(1)
    gated = (gate[:, :EARLY].astype(F32) * grad[:, :EARLY].astype(F32)).astype(jnp.bfloat16)
    arrived = passed_along(gated, "section", -1)
    gate, grad, gated = lax.optimization_barrier((gate, grad, gated))
    local, full, sums = as_one_step(always, late_step, gate, grad, decay, gain)
    late_rows = passed_along(local, "section", -1)
    out, entries, params = as_one_step(always, early_step, plane, arrived, full, sums)
    return finish_late(out, late_rows, entries, params)[None]


def solution(mesh):
    sections = mesh.shape["section"]
    parts = Mesh(mesh.devices.reshape(PLANES, PLACES, sections), ("plane", "place", "section"))
    rows = P("section", ("plane", "place"), None)
    params = P("section", None, None)
    return jax.shard_map(
        shards,
        mesh=parts,
        in_specs=(rows, rows, params, params),
        out_specs=rows,
        check_vma=False,
    )
```

```python
import functools

import jax
import jax.numpy as jnp
from jax import lax
from jax.experimental import pallas as pl
from jax.experimental.pallas import tpu as pltpu
from jax.sharding import Mesh, PartitionSpec as P

MODES = 16
ROWS = 128
PLACES = 8
SLOT = MODES // PLACES
PLANES = 64 // PLACES
EARLY = 2048
WIDTH = 1024
HALF = PLANES // 2
F32 = jnp.float32


def gated_rows(gate, grad):
    return (gate.astype(F32) * grad.astype(F32)).astype(jnp.bfloat16).astype(F32)


def lanes_of(group):
    return pl.ds(pl.multiple_of(group * 128, 128), 128)


def mode_row(ref, j, lanes):
    row = ref[j : j + 1, lanes] if len(ref.shape) == 2 else ref[j // SLOT, j % SLOT : j % SLOT + 1, lanes]
    return jnp.broadcast_to(row, (8, 128))


def outer_rows(ref, lanes):
    parts = ref[:, :, lanes].astype(F32)
    chips = [parts[2 * c] + parts[2 * c + 1] for c in range(PLACES // 2)]
    return [
        jnp.broadcast_to(chips[j // (2 * SLOT)][j % (2 * SLOT)][None], (8, 128))
        for j in range(MODES)
    ]


def source_rows(refs, rows, lanes):
    if len(refs) == 1:
        return refs[0][rows, lanes].astype(F32)
    return gated_rows(refs[0][rows, lanes], refs[1][rows, lanes])


def columns(shape, first=0):
    lead = (0,) * (len(shape) - 1)
    skip = first // WIDTH
    return pl.BlockSpec(shape[:-1] + (WIDTH,), lambda c: lead + (c + skip,))


def in_parts(kernel, sources, counts):
    def body(*refs):
        if len(counts) == 1:
            return kernel(refs[:sources], *refs[sources:])
        step, start = pl.program_id(0), 0
        for source, count in zip(refs[:sources], counts):
            pl.when((step >= start) & (step < start + count))(
                functools.partial(kernel, (source,), *refs[sources:])
            )
            start += count

    return body


def part_columns(parts):
    specs, start = [], 0
    for part in parts:
        count = part.shape[1] // WIDTH
        specs.append(
            pl.BlockSpec(
                (ROWS, WIDTH), lambda c, s=start, n=count: (0, jnp.clip(c - s, 0, n - 1))
            )
        )
        start += count
    return specs, [part.shape[1] // WIDTH for part in parts]


def state_kernel(sources, decay_ref, state_ref):
    sub = lax.broadcasted_iota(jnp.int32, (8, 128), 0).astype(F32)

    def one_group(group, _):
        lanes = lanes_of(group)
        rates = [mode_row(decay_ref, j, lanes) for j in range(MODES)]
        leap = [jnp.exp(-8.0 * r) for r in rates]
        held = [None] * MODES
        for pair in reversed(range(ROWS // 16)):
            both = source_rows(sources, slice(16 * pair, 16 * pair + 16), lanes)
            for part in (both[8:16], both[0:8]):
                held = [part if h is None else h * q + part for h, q in zip(held, leap)]
        for j in range(MODES):
            total = jnp.sum(held[j] * jnp.exp(-rates[j] * sub), axis=0, keepdims=True)
            state_ref[j // SLOT, j % SLOT : j % SLOT + 1, lanes] = total
        return 0

    lax.fori_loop(0, state_ref.shape[2] // 128, one_group, 0)


def all_states(gate, grad, decay, width=1024):
    channels = gate.shape[1]
    wide = lambda c: (0, c)
    return pl.pallas_call(
        in_parts(state_kernel, 2, [1]),
        grid=(channels // width,),
        in_specs=[pl.BlockSpec((n, width), wide) for n in (ROWS, ROWS, MODES)],
        out_specs=pl.BlockSpec((PLACES, SLOT, width), lambda c: (0, 0, c)),
        out_shape=jax.ShapeDtypeStruct((PLACES, SLOT, channels), F32),
        name="all_states",
    )(gate, grad, decay)


def early_states(parts, decay, decay_first):
    specs, counts = part_columns(parts)
    return pl.pallas_call(
        in_parts(state_kernel, len(parts), counts),
        grid=(sum(counts),),
        in_specs=specs + [columns(decay.shape, decay_first)],
        out_specs=columns((PLACES, SLOT, EARLY)),
        out_shape=jax.ShapeDtypeStruct((PLACES, SLOT, EARLY), F32),
        name="early_states",
    )(*parts, decay)


def plane_kernel(state_ref, rate_ref, gain_ref, out_ref):
    late = rate_ref.shape[1] - EARLY
    step = jnp.exp(-float(ROWS) * rate_ref[...])
    total = jnp.zeros_like(step)
    for k in reversed(range(PLACES)):
        out_ref[k, :, :late] = total[:, EARLY:]
        total = total * step + state_ref[k]
    total = total * gain_ref[...]
    for k in range(PLACES):
        out_ref[k, :, late:] = total


def plane_sums(states, rates, gains):
    channels = rates.shape[1]
    return pl.pallas_call(
        plane_kernel,
        out_shape=jax.ShapeDtypeStruct((PLACES, SLOT, 2 * channels - EARLY), F32),
        name="plane_sums",
    )(states, rates, gains)


def inner_kernel(state_ref, param_ref, entry_ref):
    step = jnp.exp(-float(ROWS) * param_ref[:, :EARLY])
    total = jnp.zeros_like(step)
    for k in reversed(range(PLACES)):
        entry_ref[k] = total
        total = total * step + state_ref[k]


def inner_entries(states, params):
    return pl.pallas_call(
        inner_kernel,
        out_shape=jax.ShapeDtypeStruct(states.shape, F32),
        name="inner_entries",
    )(states, params)


def outer_kernel(core_ref, rate_ref, *refs):
    sum_refs, entry_ref = refs[:-1], refs[-1]
    rates = rate_ref[...]
    stride = jnp.exp(-float(ROWS * PLACES) * rates)
    carry = sum_refs[-1][...].astype(F32)
    for sum_ref in sum_refs[-2::-1]:
        carry = carry * stride + sum_ref[...].astype(F32)
    beyond = jnp.exp(-float(ROWS * PLACES * HALF) * rates)
    carry = jnp.where(core_ref[0] == 0, carry, carry * beyond)
    step = jnp.exp(-float(ROWS) * rates)
    for k in reversed(range(PLACES)):
        entry_ref[k] = carry.astype(jnp.bfloat16)
        carry = carry * step


def outer_entries(core, rates, sums):
    whole = pl.BlockSpec(memory_space=pltpu.VMEM)
    return pl.pallas_call(
        outer_kernel,
        in_specs=[pl.BlockSpec(memory_space=pltpu.SMEM)] + [whole] * (1 + len(sums)),
        out_shape=jax.ShapeDtypeStruct((PLACES,) + rates.shape, jnp.bfloat16),
        name="outer_entries",
    )(core, rates, *sums)


def sweep_kernel(sources, entry_ref, decay_ref, gain_ref, out_ref, source, result):
    sub = lax.broadcasted_iota(jnp.int32, (8, 128), 0)

    def one_group(group, _):
        lanes = lanes_of(group)
        for pair in range(ROWS // 16):
            rows = slice(16 * pair, 16 * pair + 16)
            source[rows, :] = source_rows(sources, rows, lanes)
        rates = [mode_row(decay_ref, j, lanes) for j in range(MODES)]
        keep = [jnp.exp(-r) for r in rates]
        held = [None] * MODES
        for i in reversed(range(16)):
            part = source[pl.ds(i, 8, stride=16), :]
            held = [part if h is None else h * q + part for h, q in zip(held, keep)]
        for j in range(MODES):
            value = jnp.where(sub == 7, mode_row(entry_ref, j, lanes), pltpu.roll(held[j], 7, 0))
            for shift in (1, 2, 4):
                leap = jnp.where(sub < 8 - shift, jnp.exp(-16.0 * shift * rates[j]), 0.0)
                value = value + leap * pltpu.roll(value, 8 - shift, 0)
            held[j] = value
        gains = [mode_row(gain_ref, j, lanes) for j in range(MODES)]
        for i in reversed(range(16)):
            part = source[pl.ds(i, 8, stride=16), :]
            held = [h * q + part for h, q in zip(held, keep)]
            terms = [h * a for h, a in zip(held, gains)]
            while len(terms) > 1:
                terms = [a + b for a, b in zip(terms[::2], terms[1::2])]
            result[pl.ds(i, 8, stride=16), :] = terms[0]
        for pair in range(ROWS // 16):
            rows = slice(16 * pair, 16 * pair + 16)
            out_ref[rows, lanes] = result[rows, :].astype(jnp.bfloat16)
        return 0

    lax.fori_loop(0, WIDTH // 128, one_group, 0)


def sweep(sources, specs, counts, params, channels):
    return pl.pallas_call(
        in_parts(sweep_kernel, len(sources), counts),
        grid=(channels // WIDTH,),
        in_specs=specs + [columns(a.shape, first) for a, first in params],
        out_specs=columns((ROWS, channels)),
        out_shape=jax.ShapeDtypeStruct((ROWS, channels), jnp.bfloat16),
        scratch_shapes=[pltpu.VMEM((ROWS, 128), F32), pltpu.VMEM((ROWS, 128), F32)],
        name="sweep",
    )(*sources, *(a for a, _ in params))


def finish_kernel(sources, entry_ref, decay_ref, out_ref):
    ahead = 8.0 - lax.broadcasted_iota(jnp.int32, (8, 128), 0).astype(F32)

    def one_group(group, _):
        lanes = lanes_of(group)
        rates = [mode_row(decay_ref, j, lanes) for j in range(MODES)]
        leap = [jnp.exp(-8.0 * r) for r in rates]
        enter = outer_rows(entry_ref, lanes)
        held = [e * jnp.exp(-r * ahead) for e, r in zip(enter, rates)]
        for pair in reversed(range(ROWS // 16)):
            rows = slice(16 * pair, 16 * pair + 16)
            halves = []
            for _ in range(2):
                terms = held
                while len(terms) > 1:
                    terms = [a + b for a, b in zip(terms[::2], terms[1::2])]
                halves.append(terms[0])
                held = [h * q for h, q in zip(held, leap)]
            whole = jnp.concatenate(halves[::-1], axis=0)
            out_ref[rows, lanes] = (source_rows(sources, rows, lanes) + whole).astype(jnp.bfloat16)
        return 0

    lax.fori_loop(0, WIDTH // 128, one_group, 0)


def finish(parts, entries, decay):
    specs, counts = part_columns(parts)
    channels = entries.shape[2]
    return pl.pallas_call(
        in_parts(finish_kernel, len(parts), counts),
        grid=(sum(counts),),
        in_specs=specs + [columns(entries.shape), columns((PLACES, SLOT, channels))],
        out_specs=columns((ROWS, channels)),
        out_shape=pltpu.HBM((ROWS, channels), jnp.bfloat16),
        name="finish",
    )(*parts, entries, decay)


def exchange(values, axis):
    return lax.all_to_all(values, axis, split_axis=0, concat_axis=0, tiled=True)


def passed_along(shard, axis, by):
    count = lax.axis_size(axis)
    return lax.ppermute(shard, axis, [(i, (i + by) % count) for i in range(count)])


def as_one_step(always, step, *args):
    shapes = jax.eval_shape(step, *args)
    empty = lambda *_: jax.tree.map(lambda a: jnp.zeros(a.shape, a.dtype), shapes)
    return lax.cond(always, step, empty, *args)


def half_ring(message):
    planes, sections = lax.axis_size("plane"), lax.axis_size("section")
    pairs = [
        (z * sections + s, (z + HALF) % planes * sections + (s - 1) % sections)
        for z in range(planes)
        for s in range(sections)
    ]
    return lax.ppermute(message, ("plane", "section"), pairs)


def from_later(sums, near):
    sections = lax.axis_size("section")
    number = lambda z, k, s: (z * PLACES + k) * sections + s % sections
    pairs = [
        (number(z, k, s), number(z - near - k % 2 * HALF, k, s - 1))
        for k in range(PLACES)
        for z in range(near + k % 2 * HALF, PLANES)
        for s in range(sections)
    ]
    return lax.ppermute(sums, ("plane", "place", "section"), pairs)


def late_step(gate, grad, decay, gain, rates, gains):
    channels = gate.shape[1]
    late = channels - EARLY
    states = exchange(all_states(gate, grad, decay), "place")
    spread = exchange(plane_sums(states, rates, gains), "place")
    chip = lax.axis_index("place") // 2 * 2
    sums = lax.dynamic_slice(spread, (chip, 0, late), (2, SLOT, channels))
    sums = sums.reshape(2 * SLOT, channels).astype(jnp.bfloat16)
    sources = [gate, grad]
    specs = [columns(s.shape, EARLY) for s in sources]
    inputs = [(spread, 0), (decay, EARLY), (gain, EARLY)]
    return sweep(sources, specs, [1], inputs, late), sums


def early_step(gated, params, sums):
    specs, counts = part_columns([gated])
    channels = params.shape[1] - EARLY
    sums = [from_later(sums, k) for k in range(1, HALF + 1)]
    everywhere = exchange(jnp.broadcast_to(params[None], (PLACES,) + params.shape), "place")
    states = exchange(early_states([gated], everywhere, 0), "place")
    entries = exchange(inner_entries(states, params), "place")
    inputs = [(entries, 0), (everywhere, 0), (everywhere, channels)]
    chip = lax.axis_index("place") // 2 * 2
    rates = lax.dynamic_slice(everywhere, (chip, 0, 0), (2, SLOT, channels))
    rates = rates.reshape(2 * SLOT, channels)
    return sweep([gated], specs, counts, inputs, EARLY), everywhere, rates, sums


def last_step(core, rates, sums):
    return exchange(outer_entries(core, rates, sums), "place")


def shards(gate, grad, decay, amplitude):
    gate, grad, decay, gain = gate[0], grad[0], decay[0], amplitude[0]
    place = lax.axis_index("place")
    always = place >= 0
    core = (place % 2).reshape(1)
    rates = lax.dynamic_slice_in_dim(decay, SLOT * place, SLOT, axis=0)
    gains = lax.dynamic_slice_in_dim(gain, SLOT * place, SLOT, axis=0)
    params = half_ring(jnp.concatenate([rates, gains[:, :EARLY]], axis=1))
    gated = (gate[:, :EARLY].astype(F32) * grad[:, :EARLY].astype(F32)).astype(jnp.bfloat16)
    arrived = passed_along(gated, "section", -1)
    gate, grad, gated, params = lax.optimization_barrier((gate, grad, gated, params))
    local, sums = as_one_step(always, late_step, gate, grad, decay, gain, rates, gains)
    late_rows = passed_along(local, "section", -1)
    early_rows, everywhere, rates, sums = as_one_step(
        always, early_step, arrived, params, sums
    )
    entries = as_one_step(always, last_step, core, rates, sums)
    return finish([early_rows, late_rows], entries, everywhere)[None]


def solution(mesh):
    sections = mesh.shape["section"]
    parts = Mesh(mesh.devices.reshape(PLANES, PLACES, sections), ("plane", "place", "section"))
    rows = P("section", ("plane", "place"), None)
    params = P("section", None, None)
    return jax.shard_map(
        shards,
        mesh=parts,
        in_specs=(rows, rows, params, params),
        out_specs=rows,
        check_vma=False,
    )
```

```python
import functools

import jax
import jax.numpy as jnp
from jax import lax
from jax.experimental import pallas as pl
from jax.experimental.pallas import tpu as pltpu
from jax.sharding import Mesh, PartitionSpec as P

MODES = 16
ROWS = 128
PLACES = 8
SLOT = MODES // PLACES
PLANES = 64 // PLACES
EARLY = 2048
WIDTH = 1024
HALF = PLANES // 2
F32 = jnp.float32


def gated_rows(gate, grad):
    return (gate.astype(F32) * grad.astype(F32)).astype(jnp.bfloat16).astype(F32)


def lanes_of(group):
    return pl.ds(pl.multiple_of(group * 128, 128), 128)


def mode_row(ref, j, lanes):
    row = ref[j : j + 1, lanes] if len(ref.shape) == 2 else ref[j // SLOT, j % SLOT : j % SLOT + 1, lanes]
    return jnp.broadcast_to(row, (8, 128))


def outer_rows(ref, lanes):
    parts = ref[:, :, lanes].astype(F32)
    chips = [parts[2 * c] + parts[2 * c + 1] for c in range(PLACES // 2)]
    return [
        jnp.broadcast_to(chips[j // (2 * SLOT)][j % (2 * SLOT)][None], (8, 128))
        for j in range(MODES)
    ]


def source_rows(refs, rows, lanes):
    if len(refs) == 1:
        return refs[0][rows, lanes].astype(F32)
    return gated_rows(refs[0][rows, lanes], refs[1][rows, lanes])


def columns(shape, first=0):
    lead = (0,) * (len(shape) - 1)
    skip = first // WIDTH
    return pl.BlockSpec(shape[:-1] + (WIDTH,), lambda c: lead + (c + skip,))


def in_parts(kernel, sources, counts):
    def body(*refs):
        if len(counts) == 1:
            return kernel(refs[:sources], *refs[sources:])
        step, start = pl.program_id(0), 0
        for source, count in zip(refs[:sources], counts):
            pl.when((step >= start) & (step < start + count))(
                functools.partial(kernel, (source,), *refs[sources:])
            )
            start += count

    return body


def part_columns(parts):
    specs, start = [], 0
    for part in parts:
        count = part.shape[1] // WIDTH
        specs.append(
            pl.BlockSpec(
                (ROWS, WIDTH), lambda c, s=start, n=count: (0, jnp.clip(c - s, 0, n - 1))
            )
        )
        start += count
    return specs, [part.shape[1] // WIDTH for part in parts]


def state_kernel(sources, decay_ref, state_ref):
    sub = lax.broadcasted_iota(jnp.int32, (8, 128), 0).astype(F32)

    def one_group(group, _):
        lanes = lanes_of(group)
        rates = [mode_row(decay_ref, j, lanes) for j in range(MODES)]
        leap = [jnp.exp(-8.0 * r) for r in rates]
        held = [None] * MODES
        for pair in reversed(range(ROWS // 16)):
            both = source_rows(sources, slice(16 * pair, 16 * pair + 16), lanes)
            for part in (both[8:16], both[0:8]):
                held = [part if h is None else h * q + part for h, q in zip(held, leap)]
        for j in range(MODES):
            total = jnp.sum(held[j] * jnp.exp(-rates[j] * sub), axis=0, keepdims=True)
            state_ref[j // SLOT, j % SLOT : j % SLOT + 1, lanes] = total
        return 0

    lax.fori_loop(0, state_ref.shape[2] // 128, one_group, 0)


def all_states(gate, grad, decay, width=1024):
    channels = gate.shape[1]
    wide = lambda c: (0, c)
    return pl.pallas_call(
        in_parts(state_kernel, 2, [1]),
        grid=(channels // width,),
        in_specs=[pl.BlockSpec((n, width), wide) for n in (ROWS, ROWS, MODES)],
        out_specs=pl.BlockSpec((PLACES, SLOT, width), lambda c: (0, 0, c)),
        out_shape=jax.ShapeDtypeStruct((PLACES, SLOT, channels), F32),
        name="all_states",
    )(gate, grad, decay)


def early_states(parts, decay, decay_first):
    specs, counts = part_columns(parts)
    return pl.pallas_call(
        in_parts(state_kernel, len(parts), counts),
        grid=(sum(counts),),
        in_specs=specs + [columns(decay.shape, decay_first)],
        out_specs=columns((PLACES, SLOT, EARLY)),
        out_shape=jax.ShapeDtypeStruct((PLACES, SLOT, EARLY), F32),
        name="early_states",
    )(*parts, decay)


def plane_kernel(state_ref, rate_ref, gain_ref, out_ref):
    late = rate_ref.shape[1] - EARLY
    step = jnp.exp(-float(ROWS) * rate_ref[...])
    total = jnp.zeros_like(step)
    for k in reversed(range(PLACES)):
        out_ref[k, :, :late] = total[:, EARLY:]
        total = total * step + state_ref[k]
    total = total * gain_ref[...]
    for k in range(PLACES):
        out_ref[k, :, late:] = total


def plane_sums(states, rates, gains):
    channels = rates.shape[1]
    return pl.pallas_call(
        plane_kernel,
        out_shape=jax.ShapeDtypeStruct((PLACES, SLOT, 2 * channels - EARLY), F32),
        name="plane_sums",
    )(states, rates, gains)


def entry_kernel(core_ref, rate_ref, param_ref, state_ref, *refs):
    sum_refs, entry_ref = refs[:-1], refs[-1]
    first = core_ref[0] == 0
    rates = rate_ref[...]
    stride = jnp.exp(-float(ROWS * PLACES) * rates)
    carry = sum_refs[-1][...].astype(F32)
    for sum_ref in sum_refs[-2::-1]:
        carry = carry * stride + sum_ref[...].astype(F32)
    beyond = jnp.exp(-float(ROWS * PLACES * HALF) * rates)
    carry = jnp.where(first, carry, carry * beyond)
    step = jnp.exp(-float(ROWS) * rates)
    gains = param_ref[:, rates.shape[1] :]
    early, late = carry[:, :EARLY], carry[:, EARLY:]
    for k in reversed(range(PLACES)):
        entry_ref[k, :, :EARLY] = early.astype(jnp.bfloat16)
        entry_ref[k, :, EARLY:] = late.astype(jnp.bfloat16)
        own = state_ref[k] * gains
        own = jnp.concatenate([jnp.where(first, own, 0.0), jnp.where(first, 0.0, own)], axis=0)
        early = early * step[:, :EARLY] + own
        late = late * step[:, EARLY:]


def block_entries(core, rates, params, states, sums):
    whole = pl.BlockSpec(memory_space=pltpu.VMEM)
    return pl.pallas_call(
        entry_kernel,
        in_specs=[pl.BlockSpec(memory_space=pltpu.SMEM)] + [whole] * (3 + len(sums)),
        out_shape=jax.ShapeDtypeStruct((PLACES,) + rates.shape, jnp.bfloat16),
        name="block_entries",
    )(core, rates, params, states, *sums)


def sweep_kernel(sources, *refs):
    entry_refs, (decay_ref, gain_ref, out_ref, source, result) = refs[:-5], refs[-5:]
    sub = lax.broadcasted_iota(jnp.int32, (8, 128), 0)

    def one_group(group, _):
        lanes = lanes_of(group)
        for pair in range(ROWS // 16):
            rows = slice(16 * pair, 16 * pair + 16)
            source[rows, :] = source_rows(sources, rows, lanes)
        rates = [mode_row(decay_ref, j, lanes) for j in range(MODES)]
        keep = [jnp.exp(-r) for r in rates]
        held = [None] * MODES
        for i in reversed(range(16)):
            part = source[pl.ds(i, 8, stride=16), :]
            held = [part if h is None else h * q + part for h, q in zip(held, keep)]
        for j in range(MODES):
            enter = mode_row(entry_refs[0], j, lanes) if entry_refs else 0.0
            value = jnp.where(sub == 7, enter, pltpu.roll(held[j], 7, 0))
            for shift in (1, 2, 4):
                leap = jnp.where(sub < 8 - shift, jnp.exp(-16.0 * shift * rates[j]), 0.0)
                value = value + leap * pltpu.roll(value, 8 - shift, 0)
            held[j] = value
        gains = [mode_row(gain_ref, j, lanes) for j in range(MODES)]
        for i in reversed(range(16)):
            part = source[pl.ds(i, 8, stride=16), :]
            held = [h * q + part for h, q in zip(held, keep)]
            terms = [h * a for h, a in zip(held, gains)]
            while len(terms) > 1:
                terms = [a + b for a, b in zip(terms[::2], terms[1::2])]
            result[pl.ds(i, 8, stride=16), :] = terms[0]
        for pair in range(ROWS // 16):
            rows = slice(16 * pair, 16 * pair + 16)
            out_ref[rows, lanes] = result[rows, :].astype(jnp.bfloat16)
        return 0

    lax.fori_loop(0, WIDTH // 128, one_group, 0)


def sweep(sources, specs, counts, params, channels):
    return pl.pallas_call(
        in_parts(sweep_kernel, len(sources), counts),
        grid=(channels // WIDTH,),
        in_specs=specs + [columns(a.shape, first) for a, first in params],
        out_specs=columns((ROWS, channels)),
        out_shape=jax.ShapeDtypeStruct((ROWS, channels), jnp.bfloat16),
        scratch_shapes=[pltpu.VMEM((ROWS, 128), F32), pltpu.VMEM((ROWS, 128), F32)],
        name="sweep",
    )(*sources, *(a for a, _ in params))


def finish_kernel(sources, entry_ref, decay_ref, out_ref):
    ahead = 8.0 - lax.broadcasted_iota(jnp.int32, (8, 128), 0).astype(F32)

    def one_group(group, _):
        lanes = lanes_of(group)
        rates = [mode_row(decay_ref, j, lanes) for j in range(MODES)]
        leap = [jnp.exp(-8.0 * r) for r in rates]
        enter = outer_rows(entry_ref, lanes)
        held = [e * jnp.exp(-r * ahead) for e, r in zip(enter, rates)]
        for pair in reversed(range(ROWS // 16)):
            rows = slice(16 * pair, 16 * pair + 16)
            halves = []
            for _ in range(2):
                terms = held
                while len(terms) > 1:
                    terms = [a + b for a, b in zip(terms[::2], terms[1::2])]
                halves.append(terms[0])
                held = [h * q for h, q in zip(held, leap)]
            whole = jnp.concatenate(halves[::-1], axis=0)
            out_ref[rows, lanes] = (source_rows(sources, rows, lanes) + whole).astype(jnp.bfloat16)
        return 0

    lax.fori_loop(0, WIDTH // 128, one_group, 0)


def finish(parts, entries, decay):
    specs, counts = part_columns(parts)
    channels = entries.shape[2]
    return pl.pallas_call(
        in_parts(finish_kernel, len(parts), counts),
        grid=(sum(counts),),
        in_specs=specs + [columns(entries.shape), columns((PLACES, SLOT, channels))],
        out_specs=columns((ROWS, channels)),
        out_shape=pltpu.HBM((ROWS, channels), jnp.bfloat16),
        name="finish",
    )(*parts, entries, decay)


def exchange(values, axis):
    return lax.all_to_all(values, axis, split_axis=0, concat_axis=0, tiled=True)


def passed_along(shard, axis, by):
    count = lax.axis_size(axis)
    return lax.ppermute(shard, axis, [(i, (i + by) % count) for i in range(count)])


def as_one_step(always, step, *args):
    shapes = jax.eval_shape(step, *args)
    empty = lambda *_: jax.tree.map(lambda a: jnp.zeros(a.shape, a.dtype), shapes)
    return lax.cond(always, step, empty, *args)


def half_ring(message):
    planes, sections = lax.axis_size("plane"), lax.axis_size("section")
    pairs = [
        (z * sections + s, (z + HALF) % planes * sections + (s - 1) % sections)
        for z in range(planes)
        for s in range(sections)
    ]
    return lax.ppermute(message, ("plane", "section"), pairs)


def from_later(sums, near):
    sections = lax.axis_size("section")
    number = lambda z, k, s: (z * PLACES + k) * sections + s % sections
    pairs = [
        (number(z, k, s), number(z - near - k % 2 * HALF, k, s - 1))
        for k in range(PLACES)
        for z in range(near + k % 2 * HALF, PLANES)
        for s in range(sections)
    ]
    return lax.ppermute(sums, ("plane", "place", "section"), pairs)


def late_step(gate, grad, decay, gain, rates, gains):
    channels = gate.shape[1]
    late = channels - EARLY
    states = exchange(all_states(gate, grad, decay), "place")
    spread = exchange(plane_sums(states, rates, gains), "place")
    chip = lax.axis_index("place") // 2 * 2
    sums = lax.dynamic_slice(spread, (chip, 0, late), (2, SLOT, channels))
    sums = sums.reshape(2 * SLOT, channels).astype(jnp.bfloat16)
    sources = [gate, grad]
    specs = [columns(s.shape, EARLY) for s in sources]
    inputs = [(spread, 0), (decay, EARLY), (gain, EARLY)]
    return sweep(sources, specs, [1], inputs, late), sums


def early_step(gated, params, sums):
    specs, counts = part_columns([gated])
    channels = params.shape[1] - EARLY
    sums = [from_later(sums, k) for k in range(1, HALF + 1)]
    everywhere = exchange(jnp.broadcast_to(params[None], (PLACES,) + params.shape), "place")
    states = exchange(early_states([gated], everywhere, 0), "place")
    rows = sweep([gated], specs, counts, [(everywhere, 0), (everywhere, channels)], EARLY)
    chip = lax.axis_index("place") // 2 * 2
    rates = lax.dynamic_slice(everywhere, (chip, 0, 0), (2, SLOT, channels))
    return rows, everywhere, rates.reshape(2 * SLOT, channels), states, sums


def last_step(core, rates, params, states, sums):
    return exchange(block_entries(core, rates, params, states, sums), "place")


def shards(gate, grad, decay, amplitude):
    gate, grad, decay, gain = gate[0], grad[0], decay[0], amplitude[0]
    place = lax.axis_index("place")
    always = place >= 0
    core = (place % 2).reshape(1)
    rates = lax.dynamic_slice_in_dim(decay, SLOT * place, SLOT, axis=0)
    gains = lax.dynamic_slice_in_dim(gain, SLOT * place, SLOT, axis=0)
    params = half_ring(jnp.concatenate([rates, gains[:, :EARLY]], axis=1))
    gated = (gate[:, :EARLY].astype(F32) * grad[:, :EARLY].astype(F32)).astype(jnp.bfloat16)
    arrived = passed_along(gated, "section", -1)
    gate, grad, gated, params = lax.optimization_barrier((gate, grad, gated, params))
    local, sums = as_one_step(always, late_step, gate, grad, decay, gain, rates, gains)
    late_rows = passed_along(local, "section", -1)
    early_rows, everywhere, rates, states, sums = as_one_step(
        always, early_step, arrived, params, sums
    )
    entries = as_one_step(always, last_step, core, rates, params, states, sums)
    return finish([early_rows, late_rows], entries, everywhere)[None]


def solution(mesh):
    sections = mesh.shape["section"]
    parts = Mesh(mesh.devices.reshape(PLANES, PLACES, sections), ("plane", "place", "section"))
    rows = P("section", ("plane", "place"), None)
    params = P("section", None, None)
    return jax.shard_map(
        shards,
        mesh=parts,
        in_specs=(rows, rows, params, params),
        out_specs=rows,
        check_vma=False,
    )
```

```python
import functools

import jax
import jax.numpy as jnp
from jax import lax
from jax.experimental import pallas as pl
from jax.experimental.pallas import tpu as pltpu
from jax.sharding import Mesh, PartitionSpec as P

MODES = 16
ROWS = 128
PLACES = 8
SLOT = MODES // PLACES
PLANES = 64 // PLACES
EARLY = 2048
WIDTH = 1024
HALF = PLANES // 2
F32 = jnp.float32


def gated_rows(gate, grad):
    return (gate.astype(F32) * grad.astype(F32)).astype(jnp.bfloat16).astype(F32)


def lanes_of(group):
    return pl.ds(pl.multiple_of(group * 128, 128), 128)


def mode_row(ref, j, lanes):
    row = ref[j : j + 1, lanes] if len(ref.shape) == 2 else ref[j // SLOT, j % SLOT : j % SLOT + 1, lanes]
    return jnp.broadcast_to(row, (8, 128))


def outer_rows(ref, lanes):
    parts = ref[:, :, lanes].astype(F32)
    chips = [parts[2 * c] + parts[2 * c + 1] for c in range(PLACES // 2)]
    return [
        jnp.broadcast_to(chips[j // (2 * SLOT)][j % (2 * SLOT)][None], (8, 128))
        for j in range(MODES)
    ]


def source_rows(refs, rows, lanes):
    if len(refs) == 1:
        return refs[0][rows, lanes].astype(F32)
    return gated_rows(refs[0][rows, lanes], refs[1][rows, lanes])


def columns(shape, first=0):
    lead = (0,) * (len(shape) - 1)
    skip = first // WIDTH
    return pl.BlockSpec(shape[:-1] + (WIDTH,), lambda c: lead + (c + skip,))


def in_parts(kernel, sources, counts):
    def body(*refs):
        if len(counts) == 1:
            return kernel(refs[:sources], *refs[sources:])
        step, start = pl.program_id(0), 0
        for source, count in zip(refs[:sources], counts):
            pl.when((step >= start) & (step < start + count))(
                functools.partial(kernel, (source,), *refs[sources:])
            )
            start += count

    return body


def part_columns(parts):
    specs, start = [], 0
    for part in parts:
        count = part.shape[1] // WIDTH
        specs.append(
            pl.BlockSpec(
                (ROWS, WIDTH), lambda c, s=start, n=count: (0, jnp.clip(c - s, 0, n - 1))
            )
        )
        start += count
    return specs, [part.shape[1] // WIDTH for part in parts]


def state_kernel(sources, decay_ref, state_ref):
    sub = lax.broadcasted_iota(jnp.int32, (8, 128), 0).astype(F32)

    def one_group(group, _):
        lanes = lanes_of(group)
        rates = [mode_row(decay_ref, j, lanes) for j in range(MODES)]
        leap = [jnp.exp(-8.0 * r) for r in rates]
        held = [None] * MODES
        for pair in reversed(range(ROWS // 16)):
            both = source_rows(sources, slice(16 * pair, 16 * pair + 16), lanes)
            for part in (both[8:16], both[0:8]):
                held = [part if h is None else h * q + part for h, q in zip(held, leap)]
        for j in range(MODES):
            total = jnp.sum(held[j] * jnp.exp(-rates[j] * sub), axis=0, keepdims=True)
            state_ref[j // SLOT, j % SLOT : j % SLOT + 1, lanes] = total
        return 0

    lax.fori_loop(0, state_ref.shape[2] // 128, one_group, 0)


def all_states(gate, grad, decay, width=1024):
    channels = gate.shape[1]
    wide = lambda c: (0, c)
    return pl.pallas_call(
        in_parts(state_kernel, 2, [1]),
        grid=(channels // width,),
        in_specs=[pl.BlockSpec((n, width), wide) for n in (ROWS, ROWS, MODES)],
        out_specs=pl.BlockSpec((PLACES, SLOT, width), lambda c: (0, 0, c)),
        out_shape=jax.ShapeDtypeStruct((PLACES, SLOT, channels), F32),
        name="all_states",
    )(gate, grad, decay)


def early_states(parts, decay, decay_first):
    specs, counts = part_columns(parts)
    return pl.pallas_call(
        in_parts(state_kernel, len(parts), counts),
        grid=(sum(counts),),
        in_specs=specs + [columns(decay.shape, decay_first)],
        out_specs=columns((PLACES, SLOT, EARLY)),
        out_shape=jax.ShapeDtypeStruct((PLACES, SLOT, EARLY), F32),
        name="early_states",
    )(*parts, decay)


def plane_kernel(state_ref, rate_ref, gain_ref, out_ref):
    late = rate_ref.shape[1] - EARLY
    step = jnp.exp(-float(ROWS) * rate_ref[...])
    total = jnp.zeros_like(step)
    for k in reversed(range(PLACES)):
        out_ref[k, :, :late] = total[:, EARLY:]
        total = total * step + state_ref[k]
    total = total * gain_ref[...]
    for k in range(PLACES):
        out_ref[k, :, late:] = total


def plane_sums(states, rates, gains):
    channels = rates.shape[1]
    return pl.pallas_call(
        plane_kernel,
        out_shape=jax.ShapeDtypeStruct((PLACES, SLOT, 2 * channels - EARLY), F32),
        name="plane_sums",
    )(states, rates, gains)


def entry_kernel(core_ref, rate_ref, param_ref, state_ref, *refs):
    sum_refs, entry_ref = refs[:-1], refs[-1]
    first = core_ref[0] == 0
    rates = rate_ref[...]
    stride = jnp.exp(-float(ROWS * PLACES) * rates)
    carry = sum_refs[-1][...].astype(F32)
    for sum_ref in sum_refs[-2::-1]:
        carry = carry * stride + sum_ref[...].astype(F32)
    beyond = jnp.exp(-float(ROWS * PLACES * HALF) * rates)
    carry = jnp.where(first, carry, carry * beyond)
    step = jnp.exp(-float(ROWS) * rates)
    gains = param_ref[:, rates.shape[1] :]
    early, late = carry[:, :EARLY], carry[:, EARLY:]
    for k in reversed(range(PLACES)):
        entry_ref[k, :, :EARLY] = early.astype(jnp.bfloat16)
        entry_ref[k, :, EARLY:] = late.astype(jnp.bfloat16)
        own = state_ref[k] * gains
        own = jnp.concatenate([jnp.where(first, own, 0.0), jnp.where(first, 0.0, own)], axis=0)
        early = early * step[:, :EARLY] + own
        late = late * step[:, EARLY:]


def block_entries(core, rates, params, states, sums):
    whole = pl.BlockSpec(memory_space=pltpu.VMEM)
    return pl.pallas_call(
        entry_kernel,
        in_specs=[pl.BlockSpec(memory_space=pltpu.SMEM)] + [whole] * (3 + len(sums)),
        out_shape=jax.ShapeDtypeStruct((PLACES,) + rates.shape, jnp.bfloat16),
        name="block_entries",
    )(core, rates, params, states, *sums)


def sweep_kernel(sources, *refs):
    entry_refs, (decay_ref, gain_ref, out_ref, source, result) = refs[:-5], refs[-5:]
    sub = lax.broadcasted_iota(jnp.int32, (8, 128), 0)

    def one_group(group, _):
        lanes = lanes_of(group)
        for pair in range(ROWS // 16):
            rows = slice(16 * pair, 16 * pair + 16)
            source[rows, :] = source_rows(sources, rows, lanes)
        rates = [mode_row(decay_ref, j, lanes) for j in range(MODES)]
        keep = [jnp.exp(-r) for r in rates]
        held = [None] * MODES
        for i in reversed(range(16)):
            part = source[pl.ds(i, 8, stride=16), :]
            held = [part if h is None else h * q + part for h, q in zip(held, keep)]
        for j in range(MODES):
            enter = mode_row(entry_refs[0], j, lanes) if entry_refs else 0.0
            value = jnp.where(sub == 7, enter, pltpu.roll(held[j], 7, 0))
            for shift in (1, 2, 4):
                leap = jnp.where(sub < 8 - shift, jnp.exp(-16.0 * shift * rates[j]), 0.0)
                value = value + leap * pltpu.roll(value, 8 - shift, 0)
            held[j] = value
        gains = [mode_row(gain_ref, j, lanes) for j in range(MODES)]
        for i in reversed(range(16)):
            part = source[pl.ds(i, 8, stride=16), :]
            held = [h * q + part for h, q in zip(held, keep)]
            terms = [h * a for h, a in zip(held, gains)]
            while len(terms) > 1:
                terms = [a + b for a, b in zip(terms[::2], terms[1::2])]
            result[pl.ds(i, 8, stride=16), :] = terms[0]
        for pair in range(ROWS // 16):
            rows = slice(16 * pair, 16 * pair + 16)
            out_ref[rows, lanes] = result[rows, :].astype(jnp.bfloat16)
        return 0

    lax.fori_loop(0, WIDTH // 128, one_group, 0)


def sweep(sources, specs, counts, params, channels):
    return pl.pallas_call(
        in_parts(sweep_kernel, len(sources), counts),
        grid=(channels // WIDTH,),
        in_specs=specs + [columns(a.shape, first) for a, first in params],
        out_specs=columns((ROWS, channels)),
        out_shape=jax.ShapeDtypeStruct((ROWS, channels), jnp.bfloat16),
        scratch_shapes=[pltpu.VMEM((ROWS, 128), F32), pltpu.VMEM((ROWS, 128), F32)],
        name="sweep",
    )(*sources, *(a for a, _ in params))


def finish_kernel(sources, entry_ref, decay_ref, out_ref):
    ahead = 8.0 - lax.broadcasted_iota(jnp.int32, (8, 128), 0).astype(F32)

    def one_group(group, _):
        lanes = lanes_of(group)
        rates = [mode_row(decay_ref, j, lanes) for j in range(MODES)]
        leap = [jnp.exp(-8.0 * r) for r in rates]
        enter = outer_rows(entry_ref, lanes)
        held = [e * jnp.exp(-r * ahead) for e, r in zip(enter, rates)]
        for pair in reversed(range(ROWS // 16)):
            rows = slice(16 * pair, 16 * pair + 16)
            halves = []
            for _ in range(2):
                terms = held
                while len(terms) > 1:
                    terms = [a + b for a, b in zip(terms[::2], terms[1::2])]
                halves.append(terms[0])
                held = [h * q for h, q in zip(held, leap)]
            whole = jnp.concatenate(halves[::-1], axis=0)
            out_ref[rows, lanes] = (source_rows(sources, rows, lanes) + whole).astype(jnp.bfloat16)
        return 0

    lax.fori_loop(0, WIDTH // 128, one_group, 0)


def finish(parts, entries, decay):
    specs, counts = part_columns(parts)
    channels = entries.shape[2]
    return pl.pallas_call(
        in_parts(finish_kernel, len(parts), counts),
        grid=(sum(counts),),
        in_specs=specs + [columns(entries.shape), columns((PLACES, SLOT, channels))],
        out_specs=columns((ROWS, channels)),
        out_shape=pltpu.HBM((ROWS, channels), jnp.bfloat16),
        name="finish",
    )(*parts, entries, decay)


def exchange(values, axis):
    return lax.all_to_all(values, axis, split_axis=0, concat_axis=0, tiled=True)


def passed_along(shard, axis, by):
    count = lax.axis_size(axis)
    return lax.ppermute(shard, axis, [(i, (i + by) % count) for i in range(count)])


def as_one_step(always, step, *args):
    shapes = jax.eval_shape(step, *args)
    empty = lambda *_: jax.tree.map(lambda a: jnp.zeros(a.shape, a.dtype), shapes)
    return lax.cond(always, step, empty, *args)


def half_ring(message):
    planes, sections = lax.axis_size("plane"), lax.axis_size("section")
    pairs = [
        (z * sections + s, (z + HALF) % planes * sections + (s - 1) % sections)
        for z in range(planes)
        for s in range(sections)
    ]
    return lax.ppermute(message, ("plane", "section"), pairs)


def from_later(sums, near):
    sections = lax.axis_size("section")
    number = lambda z, k, s: (z * PLACES + k) * sections + s % sections
    pairs = [
        (number(z, k, s), number(z - near - k % 2 * HALF, k, s - 1))
        for k in range(PLACES)
        for z in range(near + k % 2 * HALF, PLANES)
        for s in range(sections)
    ]
    return lax.ppermute(sums, ("plane", "place", "section"), pairs)


def late_step(gate, grad, decay, gain, rates, gains):
    channels = gate.shape[1]
    late = channels - EARLY
    states = exchange(all_states(gate, grad, decay), "place")
    spread = exchange(plane_sums(states, rates, gains), "place")
    sources = [gate, grad]
    specs = [columns(s.shape, EARLY) for s in sources]
    inputs = [(spread, 0), (decay, EARLY), (gain, EARLY)]
    return sweep(sources, specs, [1], inputs, late), spread


def early_step(gated, params, spread):
    specs, counts = part_columns([gated])
    channels = params.shape[1] - EARLY
    chip = lax.axis_index("place") // 2 * 2
    sums = lax.dynamic_slice(spread, (chip, 0, channels - EARLY), (2, SLOT, channels))
    sums = sums.reshape(2 * SLOT, channels).astype(jnp.bfloat16)
    sums = [from_later(sums, k) for k in range(1, HALF + 1)]
    everywhere = exchange(jnp.broadcast_to(params[None], (PLACES,) + params.shape), "place")
    states = exchange(early_states([gated], everywhere, 0), "place")
    rows = sweep([gated], specs, counts, [(everywhere, 0), (everywhere, channels)], EARLY)
    rates = lax.dynamic_slice(everywhere, (chip, 0, 0), (2, SLOT, channels))
    return rows, everywhere, rates.reshape(2 * SLOT, channels), states, sums


def last_step(core, rates, params, states, sums):
    return exchange(block_entries(core, rates, params, states, sums), "place")


def shards(gate, grad, decay, amplitude):
    gate, grad, decay, gain = gate[0], grad[0], decay[0], amplitude[0]
    place = lax.axis_index("place")
    always = place >= 0
    core = (place % 2).reshape(1)
    rates = lax.dynamic_slice_in_dim(decay, SLOT * place, SLOT, axis=0)
    gains = lax.dynamic_slice_in_dim(gain, SLOT * place, SLOT, axis=0)
    params = half_ring(jnp.concatenate([rates, gains[:, :EARLY]], axis=1))
    gated = (gate[:, :EARLY].astype(F32) * grad[:, :EARLY].astype(F32)).astype(jnp.bfloat16)
    arrived = passed_along(gated, "section", -1)
    gate, grad, gated, params = lax.optimization_barrier((gate, grad, gated, params))
    local, spread = as_one_step(always, late_step, gate, grad, decay, gain, rates, gains)
    late_rows = passed_along(local, "section", -1)
    early_rows, everywhere, rates, states, sums = as_one_step(
        always, early_step, arrived, params, spread
    )
    entries = as_one_step(always, last_step, core, rates, params, states, sums)
    return finish([early_rows, late_rows], entries, everywhere)[None]


def solution(mesh):
    sections = mesh.shape["section"]
    parts = Mesh(mesh.devices.reshape(PLANES, PLACES, sections), ("plane", "place", "section"))
    rows = P("section", ("plane", "place"), None)
    params = P("section", None, None)
    return jax.shard_map(
        shards,
        mesh=parts,
        in_specs=(rows, rows, params, params),
        out_specs=rows,
        check_vma=False,
    )
```

```python
import functools

import jax
import jax.numpy as jnp
from jax import lax
from jax.experimental import pallas as pl
from jax.experimental.pallas import tpu as pltpu
from jax.sharding import Mesh, PartitionSpec as P

MODES = 16
ROWS = 128
PLACES = 8
SLOT = MODES // PLACES
PLANES = 64 // PLACES
EARLY = 2048
WIDTH = 1024
HALF = PLANES // 2
F32 = jnp.float32


def gated_rows(gate, grad):
    return (gate.astype(F32) * grad.astype(F32)).astype(jnp.bfloat16).astype(F32)


def lanes_of(group):
    return pl.ds(pl.multiple_of(group * 128, 128), 128)


def mode_row(ref, j, lanes):
    row = ref[j : j + 1, lanes] if len(ref.shape) == 2 else ref[j // SLOT, j % SLOT : j % SLOT + 1, lanes]
    return jnp.broadcast_to(row, (8, 128))


def outer_rows(ref, lanes):
    parts = ref[:, :, lanes].astype(F32)
    chips = [parts[2 * c] + parts[2 * c + 1] for c in range(PLACES // 2)]
    return [
        jnp.broadcast_to(chips[j // (2 * SLOT)][j % (2 * SLOT)][None], (8, 128))
        for j in range(MODES)
    ]


def source_rows(refs, rows, lanes):
    if len(refs) == 1:
        return refs[0][rows, lanes].astype(F32)
    return gated_rows(refs[0][rows, lanes], refs[1][rows, lanes])


def columns(shape, first=0):
    lead = (0,) * (len(shape) - 1)
    skip = first // WIDTH
    return pl.BlockSpec(shape[:-1] + (WIDTH,), lambda c: lead + (c + skip,))


def in_parts(kernel, sources, counts):
    def body(*refs):
        if len(counts) == 1:
            return kernel(refs[:sources], *refs[sources:])
        step, start = pl.program_id(0), 0
        for source, count in zip(refs[:sources], counts):
            pl.when((step >= start) & (step < start + count))(
                functools.partial(kernel, (source,), *refs[sources:])
            )
            start += count

    return body


def part_columns(parts):
    specs, start = [], 0
    for part in parts:
        count = part.shape[1] // WIDTH
        specs.append(
            pl.BlockSpec(
                (ROWS, WIDTH), lambda c, s=start, n=count: (0, jnp.clip(c - s, 0, n - 1))
            )
        )
        start += count
    return specs, [part.shape[1] // WIDTH for part in parts]


def state_kernel(sources, decay_ref, state_ref):
    sub = lax.broadcasted_iota(jnp.int32, (8, 128), 0).astype(F32)

    def one_group(group, _):
        lanes = lanes_of(group)
        rates = [mode_row(decay_ref, j, lanes) for j in range(MODES)]
        leap = [jnp.exp(-8.0 * r) for r in rates]
        held = [None] * MODES
        for pair in reversed(range(ROWS // 16)):
            both = source_rows(sources, slice(16 * pair, 16 * pair + 16), lanes)
            for part in (both[8:16], both[0:8]):
                held = [part if h is None else h * q + part for h, q in zip(held, leap)]
        for j in range(MODES):
            total = jnp.sum(held[j] * jnp.exp(-rates[j] * sub), axis=0, keepdims=True)
            state_ref[j // SLOT, j % SLOT : j % SLOT + 1, lanes] = total
        return 0

    lax.fori_loop(0, state_ref.shape[2] // 128, one_group, 0)


def all_states(gate, grad, decay, width=1024):
    channels = gate.shape[1]
    wide = lambda c: (0, c)
    return pl.pallas_call(
        in_parts(state_kernel, 2, [1]),
        grid=(channels // width,),
        in_specs=[pl.BlockSpec((n, width), wide) for n in (ROWS, ROWS, MODES)],
        out_specs=pl.BlockSpec((PLACES, SLOT, width), lambda c: (0, 0, c)),
        out_shape=jax.ShapeDtypeStruct((PLACES, SLOT, channels), F32),
        name="all_states",
    )(gate, grad, decay)


def early_states(parts, decay, decay_first):
    specs, counts = part_columns(parts)
    return pl.pallas_call(
        in_parts(state_kernel, len(parts), counts),
        grid=(sum(counts),),
        in_specs=specs + [columns(decay.shape, decay_first)],
        out_specs=columns((PLACES, SLOT, EARLY)),
        out_shape=jax.ShapeDtypeStruct((PLACES, SLOT, EARLY), F32),
        name="early_states",
    )(*parts, decay)


def plane_kernel(state_ref, rate_ref, gain_ref, out_ref):
    late = rate_ref.shape[1] - EARLY
    step = jnp.exp(-float(ROWS) * rate_ref[...])
    total = jnp.zeros_like(step)
    for k in reversed(range(PLACES)):
        out_ref[k, :, :late] = total[:, EARLY:]
        total = total * step + state_ref[k]
    total = total * gain_ref[...]
    for k in range(PLACES):
        out_ref[k, :, late:] = total


def plane_sums(states, rates, gains):
    channels = rates.shape[1]
    return pl.pallas_call(
        plane_kernel,
        out_shape=jax.ShapeDtypeStruct((PLACES, SLOT, 2 * channels - EARLY), F32),
        name="plane_sums",
    )(states, rates, gains)


def entry_kernel(core_ref, rate_ref, param_ref, state_ref, *refs):
    sum_refs, entry_ref = refs[:-1], refs[-1]
    first = core_ref[0] == 0
    rates = rate_ref[...]
    stride = jnp.exp(-float(ROWS * PLACES) * rates)
    carry = sum_refs[-1][...].astype(F32)
    for sum_ref in sum_refs[-2::-1]:
        carry = carry * stride + sum_ref[...].astype(F32)
    beyond = jnp.exp(-float(ROWS * PLACES * HALF) * rates)
    carry = jnp.where(first, carry, carry * beyond)
    step = jnp.exp(-float(ROWS) * rates)
    gains = param_ref[:, rates.shape[1] :]
    early, late = carry[:, :EARLY], carry[:, EARLY:]
    for k in reversed(range(PLACES)):
        entry_ref[k, :, :EARLY] = early.astype(jnp.bfloat16)
        entry_ref[k, :, EARLY:] = late.astype(jnp.bfloat16)
        own = state_ref[k] * gains
        own = jnp.concatenate([jnp.where(first, own, 0.0), jnp.where(first, 0.0, own)], axis=0)
        early = early * step[:, :EARLY] + own
        late = late * step[:, EARLY:]


def block_entries(core, rates, params, states, sums):
    whole = pl.BlockSpec(memory_space=pltpu.VMEM)
    return pl.pallas_call(
        entry_kernel,
        in_specs=[pl.BlockSpec(memory_space=pltpu.SMEM)] + [whole] * (3 + len(sums)),
        out_shape=jax.ShapeDtypeStruct((PLACES,) + rates.shape, jnp.bfloat16),
        name="block_entries",
    )(core, rates, params, states, *sums)


def sweep_kernel(sources, *refs):
    entry_refs, (decay_ref, gain_ref, out_ref, source, result) = refs[:-5], refs[-5:]
    sub = lax.broadcasted_iota(jnp.int32, (8, 128), 0)

    def one_group(group, _):
        lanes = lanes_of(group)
        for pair in range(ROWS // 16):
            rows = slice(16 * pair, 16 * pair + 16)
            source[rows, :] = source_rows(sources, rows, lanes)
        rates = [mode_row(decay_ref, j, lanes) for j in range(MODES)]
        keep = [jnp.exp(-r) for r in rates]
        held = [None] * MODES
        for i in reversed(range(16)):
            part = source[pl.ds(i, 8, stride=16), :]
            held = [part if h is None else h * q + part for h, q in zip(held, keep)]
        for j in range(MODES):
            enter = mode_row(entry_refs[0], j, lanes) if entry_refs else 0.0
            value = jnp.where(sub == 7, enter, pltpu.roll(held[j], 7, 0))
            for shift in (1, 2, 4):
                leap = jnp.where(sub < 8 - shift, jnp.exp(-16.0 * shift * rates[j]), 0.0)
                value = value + leap * pltpu.roll(value, 8 - shift, 0)
            held[j] = value
        gains = [mode_row(gain_ref, j, lanes) for j in range(MODES)]
        for i in reversed(range(16)):
            part = source[pl.ds(i, 8, stride=16), :]
            held = [h * q + part for h, q in zip(held, keep)]
            terms = [h * a for h, a in zip(held, gains)]
            while len(terms) > 1:
                terms = [a + b for a, b in zip(terms[::2], terms[1::2])]
            result[pl.ds(i, 8, stride=16), :] = terms[0]
        for pair in range(ROWS // 16):
            rows = slice(16 * pair, 16 * pair + 16)
            out_ref[rows, lanes] = result[rows, :].astype(jnp.bfloat16)
        return 0

    lax.fori_loop(0, WIDTH // 128, one_group, 0)


def sweep(sources, specs, counts, params, channels):
    return pl.pallas_call(
        in_parts(sweep_kernel, len(sources), counts),
        grid=(channels // WIDTH,),
        in_specs=specs + [columns(a.shape, first) for a, first in params],
        out_specs=columns((ROWS, channels)),
        out_shape=jax.ShapeDtypeStruct((ROWS, channels), jnp.bfloat16),
        scratch_shapes=[pltpu.VMEM((ROWS, 128), F32), pltpu.VMEM((ROWS, 128), F32)],
        name="sweep",
    )(*sources, *(a for a, _ in params))


def finish_kernel(sources, entry_ref, decay_ref, out_ref):
    ahead = 8.0 - lax.broadcasted_iota(jnp.int32, (8, 128), 0).astype(F32)

    def one_group(group, _):
        lanes = lanes_of(group)
        rates = [mode_row(decay_ref, j, lanes) for j in range(MODES)]
        leap = jnp.exp(-8.0 * decay_ref[:, :, lanes])
        leap = [
            jnp.broadcast_to(leap[j // SLOT][j % SLOT][None], (8, 128)) for j in range(MODES)
        ]
        enter = outer_rows(entry_ref, lanes)
        held = [e * jnp.exp(-r * ahead) for e, r in zip(enter, rates)]
        for pair in reversed(range(ROWS // 16)):
            rows = slice(16 * pair, 16 * pair + 16)
            halves = []
            for _ in range(2):
                terms = held
                while len(terms) > 1:
                    terms = [a + b for a, b in zip(terms[::2], terms[1::2])]
                halves.append(terms[0])
                held = [h * q for h, q in zip(held, leap)]
            whole = jnp.concatenate(halves[::-1], axis=0)
            out_ref[rows, lanes] = (source_rows(sources, rows, lanes) + whole).astype(jnp.bfloat16)
        return 0

    lax.fori_loop(0, WIDTH // 128, one_group, 0)


def finish(parts, entries, decay):
    specs, counts = part_columns(parts)
    channels = entries.shape[2]
    return pl.pallas_call(
        in_parts(finish_kernel, len(parts), counts),
        grid=(sum(counts),),
        in_specs=specs + [columns(entries.shape), columns((PLACES, SLOT, channels))],
        out_specs=columns((ROWS, channels)),
        out_shape=pltpu.HBM((ROWS, channels), jnp.bfloat16),
        name="finish",
    )(*parts, entries, decay)


def exchange(values, axis):
    return lax.all_to_all(values, axis, split_axis=0, concat_axis=0, tiled=True)


def passed_along(shard, axis, by):
    count = lax.axis_size(axis)
    return lax.ppermute(shard, axis, [(i, (i + by) % count) for i in range(count)])


def as_one_step(always, step, *args):
    shapes = jax.eval_shape(step, *args)
    empty = lambda *_: jax.tree.map(lambda a: jnp.zeros(a.shape, a.dtype), shapes)
    return lax.cond(always, step, empty, *args)


def half_ring(message):
    planes, sections = lax.axis_size("plane"), lax.axis_size("section")
    pairs = [
        (z * sections + s, (z + HALF) % planes * sections + (s - 1) % sections)
        for z in range(planes)
        for s in range(sections)
    ]
    return lax.ppermute(message, ("plane", "section"), pairs)


def from_later(sums, near):
    sections = lax.axis_size("section")
    number = lambda z, k, s: (z * PLACES + k) * sections + s % sections
    pairs = [
        (number(z, k, s), number(z - near - k % 2 * HALF, k, s - 1))
        for k in range(PLACES)
        for z in range(near + k % 2 * HALF, PLANES)
        for s in range(sections)
    ]
    return lax.ppermute(sums, ("plane", "place", "section"), pairs)


def late_step(gate, grad, decay, gain, rates, gains):
    channels = gate.shape[1]
    late = channels - EARLY
    states = exchange(all_states(gate, grad, decay), "place")
    spread = exchange(plane_sums(states, rates, gains), "place")
    sources = [gate, grad]
    specs = [columns(s.shape, EARLY) for s in sources]
    inputs = [(spread, 0), (decay, EARLY), (gain, EARLY)]
    return sweep(sources, specs, [1], inputs, late), spread


def early_step(gated, params, spread):
    specs, counts = part_columns([gated])
    channels = params.shape[1] - EARLY
    chip = lax.axis_index("place") // 2 * 2
    sums = lax.dynamic_slice(spread, (chip, 0, channels - EARLY), (2, SLOT, channels))
    sums = sums.reshape(2 * SLOT, channels).astype(jnp.bfloat16)
    sums = [from_later(sums, k) for k in range(1, HALF + 1)]
    everywhere = exchange(jnp.broadcast_to(params[None], (PLACES,) + params.shape), "place")
    states = exchange(early_states([gated], everywhere, 0), "place")
    rows = sweep([gated], specs, counts, [(everywhere, 0), (everywhere, channels)], EARLY)
    rates = lax.dynamic_slice(everywhere, (chip, 0, 0), (2, SLOT, channels))
    return rows, everywhere, rates.reshape(2 * SLOT, channels), states, sums


def last_step(core, rates, params, states, sums):
    return exchange(block_entries(core, rates, params, states, sums), "place")


def shards(gate, grad, decay, amplitude):
    gate, grad, decay, gain = gate[0], grad[0], decay[0], amplitude[0]
    place = lax.axis_index("place")
    always = place >= 0
    core = (place % 2).reshape(1)
    rates = lax.dynamic_slice_in_dim(decay, SLOT * place, SLOT, axis=0)
    gains = lax.dynamic_slice_in_dim(gain, SLOT * place, SLOT, axis=0)
    params = half_ring(jnp.concatenate([rates, gains[:, :EARLY]], axis=1))
    gated = (gate[:, :EARLY].astype(F32) * grad[:, :EARLY].astype(F32)).astype(jnp.bfloat16)
    arrived = passed_along(gated, "section", -1)
    gate, grad, gated, params = lax.optimization_barrier((gate, grad, gated, params))
    local, spread = as_one_step(always, late_step, gate, grad, decay, gain, rates, gains)
    late_rows = passed_along(local, "section", -1)
    early_rows, everywhere, rates, states, sums = as_one_step(
        always, early_step, arrived, params, spread
    )
    entries = as_one_step(always, last_step, core, rates, params, states, sums)
    return finish([early_rows, late_rows], entries, everywhere)[None]


def solution(mesh):
    sections = mesh.shape["section"]
    parts = Mesh(mesh.devices.reshape(PLANES, PLACES, sections), ("plane", "place", "section"))
    rows = P("section", ("plane", "place"), None)
    params = P("section", None, None)
    return jax.shard_map(
        shards,
        mesh=parts,
        in_specs=(rows, rows, params, params),
        out_specs=rows,
        check_vma=False,
    )
```
